512 devices in a mesh: dp: 64 (over z, x), tensor: 8 (over y, core).
Axes of the slice: x: 4, y: 4, z: 16, core: 2. Of those that a mesh axis runs over, the one named last changes fastest.
Arguments:
- tokens: bfloat16 [8192, 5120], P('dp'), may hold values from -6 to 6
- w_value: bfloat16 [5120, 1024], P(None, 'tensor'), may hold values from -0.078125 to 0.078125
- b_value: bfloat16 [1024], P('tensor'), may hold values from -3 to 3
- d_values: bfloat16 [8192, 1024], P('dp', 'tensor'), may hold values from -1.1953125 to 1.1953125
- error_in: bfloat16 [327680, 1024], P('dp', 'tensor'), may hold values from -9 to 9
- q_init: float32 [1024, 32], P('tensor'), may hold values from -6 to 6
Outputs:
- values: bfloat16 [8192, 1024], P('dp', 'tensor')
- d_tokens: bfloat16 [8192, 5120], P(('dp', 'tensor'))
- error_out: bfloat16 [327680, 1024], P('dp', 'tensor')
- q_next: float32 [1024, 32], P('tensor')
- d_bias: float32 [1024], P('tensor')
The draws below stay inside these ranges and needn't reach their ends.
All inputs are finite; a program needn't handle non-finite values.
Results may differ from the reference program's by a relative error of at most 0.017.
Values may be sent and summed in bfloat16 or wider, within the bound.
A program may use at most 64 MiB of HBM per device.

```python
import jax
import jax.numpy as jnp
from jax import lax

D = 5120
HEAD = 128
RANK = 32
TOK_DEV = 128
KV_HEADS = 8
KV = 1024
TOKENS = 8192
N_DP = 64


def shard_levels(stream_key, shape, cuts, smallest, high):
    def one(dim, blocks):
        draws = jax.random.uniform(jax.random.fold_in(jax.random.fold_in(stream_key, 6), dim), (blocks,), jnp.float32, smallest / len(cuts), high / len(cuts))
        return jnp.repeat(jnp.exp(draws), shape[dim] // blocks).reshape((-1,) + (1,) * (len(shape) - dim - 1))

    gain = one(*cuts[0])
    for cut in cuts[1:]:
        gain = gain * one(*cut)
    return gain


def scatter_about(stream_key, extent, scale, reach, split=(), kind=jnp.bfloat16):
    gain = shard_levels(stream_key, extent, split, -0.22, 0.18) if split else 1.0
    entries = jax.random.normal(stream_key, extent, jnp.float32) * scale * gain
    return jnp.minimum(jnp.maximum(entries, -reach), reach).astype(kind)


def setup_inputs(seed: int = 0) -> dict:
    seeds = jax.random.split(jax.random.key(seed), 7)
    tokens = scatter_about(seeds[0], (TOKENS, D), 1.0, 6.0, ((0, 64),))
    w_value = scatter_about(seeds[1], (D, KV), D ** -0.5, 0.078125, ((1, 8),))
    b_value = scatter_about(seeds[2], (KV,), 0.5, 3.0, ((0, 8),))
    d_values = scatter_about(seeds[3], (TOKENS, KV), 0.2, 1.1953125, ((0, 64), (1, 8)))
    error_in = scatter_about(seeds[4], (D * N_DP, KV), 1.5, 9.0, ((0, 64), (1, 8)))
    q_init = scatter_about(seeds[5], (KV, RANK), 1.0, 6.0, ((0, 8),), jnp.float32)
    return {"tokens": tokens, "w_value": w_value, "b_value": b_value, "d_values": d_values, "error_in": error_in, "q_init": q_init}


def orthonormal(basis):
    gram = jnp.dot(basis.T, basis, precision=lax.Precision.HIGHEST)
    lower = jnp.linalg.cholesky(gram)
    return jax.scipy.linalg.solve_triangular(lower, basis.T, lower=True).T

def reference(tokens, w_value, b_value, d_values, error_in, q_init):
    highest = lax.Precision.HIGHEST
    values = (jnp.dot(tokens.astype(jnp.float32), w_value.astype(jnp.float32), preferred_element_type=jnp.float32) + b_value.astype(jnp.float32)).astype(jnp.bfloat16)
    w_heads = w_value.reshape(D, KV_HEADS, HEAD).transpose(1, 0, 2)
    dv_heads = d_values.reshape(TOKENS, KV_HEADS, HEAD).transpose(1, 0, 2)

    def add_head(total, pair):
        weight, grad = pair
        part = jnp.dot(grad.astype(jnp.float32), weight.T.astype(jnp.float32), preferred_element_type=jnp.float32).astype(jnp.bfloat16)
        part = lax.optimization_barrier(part)
        return (total + part.astype(jnp.float32), None)
    d_total, _ = lax.scan(add_head, jnp.zeros((TOKENS, D), jnp.float32), (w_heads, dv_heads))
    d_tokens = d_total.astype(jnp.bfloat16)
    q_heads = q_init.reshape(KV_HEADS, HEAD, RANK)
    err_sum = jnp.sum(error_in.reshape(N_DP, D, KV), axis=0, dtype=jnp.float32).reshape(D, KV_HEADS, HEAD)
    tok_full = tokens.astype(jnp.float32)
    dv_full = d_values.astype(jnp.float32).reshape(TOKENS, KV_HEADS, HEAD)
    mixed = jnp.einsum('thk,hkr->thr', dv_full, q_heads, precision=highest)
    basis = jnp.einsum('td,thr->hdr', tok_full, mixed, precision=highest)
    basis = basis + jnp.einsum('dhk,hkr->hdr', err_sum, q_heads, precision=highest)
    basis_hat = jax.vmap(orthonormal)(basis)
    projected = jnp.einsum('td,hdr->thr', tok_full, basis_hat, precision=highest)
    q_new = jnp.einsum('thk,thr->hkr', dv_full, projected, precision=highest)
    q_new = (q_new + jnp.einsum('dhk,hdr->hkr', err_sum, basis_hat, precision=highest)) / N_DP
    approx = jnp.einsum('hdr,hkr->dhk', basis_hat, q_new, precision=highest).reshape(D, KV)

    def fresh(group):
        rows, grads, memory = group
        weight_grad = lax.dot_general(rows.astype(jnp.float32), grads.astype(jnp.float32), (((0,), (0,)), ((), ())), preferred_element_type=jnp.float32)
        return (weight_grad + memory.astype(jnp.float32) - approx).astype(jnp.bfloat16)
    error_out = lax.map(fresh, (tokens.reshape(N_DP, TOK_DEV, D), d_values.reshape(N_DP, TOK_DEV, KV), error_in.reshape(N_DP, D, KV)))
    error_out = error_out.reshape(N_DP * D, KV)
    q_next = q_new.reshape(KV, RANK)
    d_bias = jnp.sum(d_values.astype(jnp.float32), axis=0) / N_DP
    return (values, d_tokens, error_out, q_next, d_bias)
```

```python
import functools

import jax
import jax.numpy as jnp
from jax import lax
from jax.experimental import pallas as pl
from jax.experimental.pallas import tpu as pltpu
from jax.sharding import PartitionSpec as P

MESH = pl.DeviceIdType.MESH
F32 = jnp.float32
BF16 = jnp.bfloat16
NX = 4
NQ = 4
NN = ((1,), (0,))
NT = ((1,), (1,))
TN = ((0,), (0,))


def dot(a, b, dims, precision=None):
    return lax.dot_general(a, b, (dims, ((), ())), preferred_element_type=F32, precision=precision)


def split(v):
    high = v.astype(BF16)
    low = (v - high.astype(F32)).astype(BF16)
    return jnp.concatenate([high, low], axis=0)


def fold(v):
    n = v.shape[0] // 2
    return v[:n] + v[n:]


def inverse_lower(gram):
    n = gram.shape[0]
    row = lax.broadcasted_iota(jnp.int32, (n, n), 0)
    col = lax.broadcasted_iota(jnp.int32, (n, n), 1)
    a = gram
    inv = (row == col).astype(F32)
    for k in range(0, n, 2):
        col0, col1 = a[:, k : k + 1], a[:, k + 1 : k + 2]
        above = a[k : k + 1, k + 1 : k + 2]
        scale0 = 1.0 / a[k : k + 1, k : k + 1]
        step = a[k + 1 : k + 2, k : k + 1] * scale0
        scale1 = 1.0 / (a[k + 1 : k + 2, k + 1 : k + 2] - step * above)
        factor0 = jnp.where(row[:, :1] > k, col0 * scale0, 0.0)
        factor1 = jnp.where(row[:, :1] > k + 1, (col1 - factor0 * above) * scale1, 0.0)

        def eliminate(v):
            row0, row1 = v[k : k + 1, :], v[k + 1 : k + 2, :]
            return v - factor0 * row0 - factor1 * (row1 - step * row0)

        a, inv = eliminate(a), eliminate(inv)
    pivots = jnp.sum(jnp.where(row == col, a, 0.0), axis=1, keepdims=True)
    return inv / jnp.sqrt(pivots)


def kernel(
    nz, ny,
    tok_h, w_h, b_h, dv_h, e_h, q_h,
    vo, dto, m, bt, back, qno, dbo,
    xv, wv, ev, dvv, qv, bv,
    bxs, bxr, own, zs, zr, bf, ms, rl, mr, mx, gs,
    tsx, trx, tz, tf, bx, bz,
    pr, po, ys, yr,
    in_sem,
    ms_s, rl_r, mr_r, gss_s, gsr_s,
    bxs_s, bxr_s, zs_s, zr_s, ags_s, agr_s, axs_s, axr_s,
    tsx_s, trx_s, tzs_s, tzr_s, tfs_s, tfr_s,
    bias_xs, bias_xr, bias_zs, bias_zr, ps_s, pr_s, ys_s, yr_s,
):
    d_model = wv.shape[0]
    dq = d_model // NX
    dh = dq // 2
    zg = nz // NQ
    replicas = nz * NX
    dp, t = lax.axis_index("dp"), lax.axis_index("tensor")
    z, x = dp // NX, dp % NX
    y, c = t // 2, t % 2
    sib = t + 1 - 2 * c

    def at_x(xx):
        return (z * NX + xx, t)

    def at_z(zz):
        return (zz * NX + x, t)

    def at_y(yy):
        return (dp, yy * 2 + c)

    def nx(d):
        return (x + d) % NX

    def nzz(d):
        return (z + d) % nz

    def nyy(d):
        return (y + d) % ny

    x_order = (2, 1, 3)
    y_order = tuple(sorted(range(1, ny), key=lambda d: -min(d, ny - d)))
    z_order = tuple(sorted(range(1, nz), key=lambda d: -min(d, nz - d)))

    loads = {}
    for i, (name, src, dst) in enumerate(
        (("dv", dv_h, dvv), ("q", q_h, qv), ("e", e_h, ev), ("x", tok_h, xv), ("w", w_h, wv), ("b", b_h, bv))
    ):
        loads[name] = pltpu.make_async_copy(src, dst, in_sem.at[i])
        loads[name].start()

    barrier = pltpu.get_barrier_semaphore()
    peers = [at_x(nx(d)) for d in x_order] + [at_z(nzz(d)) for d in z_order]
    peers += [at_y(nyy(d)) for d in y_order] + [(dp, sib)]
    for peer in peers:
        pl.semaphore_signal(barrier, inc=1, device_id=peer, device_id_type=MESH)

    def remote(src, dst, send, recv, peer):
        return pltpu.make_async_remote_copy(
            src_ref=src, dst_ref=dst, send_sem=send, recv_sem=recv, device_id=peer, device_id_type=MESH
        )

    def arrived(ref, sem, peer):
        remote(ref, ref, sem, sem, peer).wait_recv()

    sent = []

    def send(*args):
        copy = remote(*args)
        copy.start()
        sent.append(copy)

    def columns(j):
        return pl.ds(pl.multiple_of(j * dq, 128), dq)

    loads["dv"].wait()
    loads["q"].wait()
    q_pair = split(qv[...])
    mixed = fold(dot(q_pair, dvv[...], NT))
    mixed_pair = split(mixed)
    loads["e"].wait()
    loads["x"].wait()

    def local_basis(j, half):
        cols = pl.ds(pl.multiple_of(j * dq + half * dh, 128), dh)
        return fold(dot(q_pair, ev[cols, :], NT) + dot(mixed_pair, xv[:, cols], NN))

    for half in range(2):
        for d in x_order:
            bxs[d, half] = local_basis(nx(d), half).astype(BF16)
    pl.semaphore_wait(barrier, len(peers))
    for half in range(2):
        for d in x_order:
            send(
                bxs.at[d, half], bxr.at[x, half], bxs_s.at[d, half], bxr_s.at[x, half], at_x(nx(d))
            )
    for half in range(2):
        own[half] = local_basis(x, half)

    def merged(j):
        cols = columns(j)
        m[cols, :] = dot(xv[:, cols], dvv[...], TN) + ev[cols, :].astype(F32)
        return m[cols, :]

    far = merged(nx(2)).astype(BF16)
    for h, d in ((0, 1), (1, 3)):
        ms[2, h] = far[h * dh : (h + 1) * dh]
        send(ms.at[2, h], rl.at[h], ms_s.at[2, h], rl_r.at[h], at_x(nx(d)))

    owner_pos = (zg - 1) // 2 + c
    mine = z // zg
    is_owner = z % zg == owner_pos

    def to_owner(qq):
        tgt = qq * zg + owner_pos
        return tgt, remote(zs.at[qq], zr.at[z], zs_s.at[qq], zr_s.at[z], at_z(tgt))

    for half in range(2):
        total = own[half]
        for d in x_order[::-1]:
            arrived(bxr.at[nx(d), half], bxr_s.at[nx(d), half], at_x(nx(d)))
            total = total + bxr[nx(d), half].astype(F32)
        for g in range(2):
            qq = 2 * g + half
            zs[qq] = total[16 * g : 16 * g + 16].astype(BF16)
            tgt, copy = to_owner(qq)
            pl.when(z != tgt)(copy.start)

    for h, d in ((0, 1), (1, 3)):
        near = merged(nx(d)).astype(BF16)
        ms[d, 1 - h] = near[(1 - h) * dh : (2 - h) * dh]
        send(ms.at[d, 1 - h], mr.at[h, 1 - h], ms_s.at[d, 1 - h], mr_r.at[h, 1 - h], at_x(nx(d)))

    loads["w"].wait()
    for k in range(NX):
        cols = slice(k * dq, (k + 1) * dq)
        p = dot(dvv[...], wv[cols, :], NT).astype(BF16)
        for yy in range(ny):
            for cc in range(2):
                first = (2 * yy + cc) * 16
                po[yy, cc, :, cols] = p[first : first + 16]
    for yy in range(ny):
        send(po.at[yy, 1 - c], pr.at[yy], ps_s.at[yy], pr_s.at[yy], (dp, sib))
    merged(x)
    for h, d in ((0, 1), (1, 3)):
        arrived(rl.at[h], rl_r.at[h], at_x(nx(4 - d)))
        rows = pl.ds(pl.multiple_of(nx(d) * dq + h * dh, 128), dh)
        ms[d, h] = (m[rows, :] + rl[h].astype(F32)).astype(BF16)
        send(ms.at[d, h], mr.at[h, h], ms_s.at[d, h], mr_r.at[h, h], at_x(nx(d)))

    def block(qq):
        g, half = qq // 2, qq % 2
        return bf.at[x, pl.ds(pl.multiple_of(g * 16, 16), 16), pl.ds(pl.multiple_of(half * dh, 128), dh)]

    def from_owner(d):
        return remote(block(mine), block(mine), ags_s.at[d], agr_s.at[mine], at_z(nzz(d)))

    @pl.when(is_owner)
    def _():
        acc = zs[mine].astype(F32)
        for d in z_order[::-1]:
            arrived(zr.at[nzz(d)], zr_s.at[nzz(d)], at_z(nzz(d)))
            acc = acc + zr[nzz(d)].astype(F32)
        block(mine)[...] = acc.astype(BF16)
        for d in z_order:
            from_owner(d).start()

    bx[x] = jnp.sum(dvv[...].astype(F32), axis=0, keepdims=True)
    for d in x_order:
        send(bx.at[x], bx.at[x], bias_xs.at[d], bias_xr.at[x], at_x(nx(d)))

    loads["b"].wait()
    vo[...] = (dot(xv[...], wv[...], NN) + bv[...].astype(F32)).astype(BF16)

    for d in y_order + (0,):
        yy = nyy(d)
        arrived(pr.at[yy], pr_s.at[yy], (dp, sib))
        ys[yy] = (po[yy, c].astype(F32) + pr[yy].astype(F32)).astype(BF16)
        if d:
            send(ys.at[yy], yr.at[y], ys_s.at[d], yr_s.at[y], at_y(yy))

    for h in range(2):
        total = m[pl.ds(pl.multiple_of(x * dq + h * dh, 128), dh), :]
        for slot, d in ((0, 3), (1, 1)):
            arrived(mr.at[slot, h], mr_r.at[slot, h], at_x(nx(d)))
            total = total + mr[slot, h].astype(F32)
        mx[2 * h * dh : 2 * (h + 1) * dh, :] = split(total)

    for qq in range(NQ):
        tgt = qq * zg + owner_pos

        @pl.when(z != tgt)
        def _():
            arrived(block(qq), agr_s.at[qq], at_z(tgt))

    basis = bf[x]
    factor = sum(
        dot(basis[:, h * dh : (h + 1) * dh], mx[k * dh : (k + 1) * dh, :], NN) for k in range(4) for h in (k // 2,)
    )
    for j in range(NX):
        tsx[j] = factor[8 * j : 8 * j + 8]
    for d in x_order:
        send(tsx.at[nx(d)], trx.at[x], tsx_s.at[d], trx_s.at[x], at_x(nx(d)))
    trx[x] = tsx[x]
    gs[x] = dot(basis, basis, NT)
    for d in x_order:
        send(gs.at[x], gs.at[x], gss_s.at[d], gsr_s.at[x], at_x(nx(d)))
    for d in x_order:
        send(bf.at[x], bf.at[x], axs_s.at[d], axr_s.at[x], at_x(nx(d)))

    for d in x_order[::-1]:
        arrived(trx.at[nx(d)], trx_s.at[nx(d)], at_x(nx(d)))
    tz[z] = (trx[0] + trx[1]) + (trx[2] + trx[3])
    for d in z_order:
        send(tz.at[z], tz.at[z], tzs_s.at[d], tzr_s.at[z], at_z(nzz(d)))

    for d in x_order:
        arrived(bx.at[nx(d)], bias_xr.at[nx(d)], at_x(nx(d)))
    bz[z] = (bx[0] + bx[1]) + (bx[2] + bx[3])
    for d in z_order:
        send(bz.at[z], bz.at[z], bias_zs.at[d], bias_zr.at[z], at_z(nzz(d)))

    for d in x_order[::-1]:
        arrived(gs.at[nx(d)], gsr_s.at[nx(d)], at_x(nx(d)))
    gram = (gs[0] + gs[1]) + (gs[2] + gs[3])
    inv = inverse_lower(gram)
    project = jnp.concatenate([inv, dot(inv, inv, TN, lax.Precision.HIGHEST)], axis=0) / replicas

    def by_rows(j):
        b = bf[j]
        bt[columns(j), :] = jnp.concatenate([b, b], axis=0).T

    by_rows(x)
    for d in z_order[::-1]:
        arrived(tz.at[nzz(d)], tzr_s.at[nzz(d)], at_z(nzz(d)))
    total = tz[0]
    for s in range(1, nz):
        total = total + tz[s]
    tf[x] = total
    for d in x_order:
        send(tf.at[x], tf.at[x], tfs_s.at[d], tfr_s.at[x], at_x(nx(d)))

    for d in x_order[::-1]:
        arrived(bf.at[nx(d)], axr_s.at[nx(d)], at_x(nx(d)))
        by_rows(nx(d))
    acc = ys[y].astype(F32)
    for d in y_order[::-1]:
        arrived(yr.at[nyy(d)], yr_s.at[nyy(d)], at_y(nyy(d)))
        acc = acc + yr[nyy(d)].astype(F32)
    dto[...] = acc.astype(BF16)
    for d in z_order[::-1]:
        arrived(bz.at[nzz(d)], bias_zr.at[nzz(d)], at_z(nzz(d)))
    total = bz[0]
    for s in range(1, nz):
        total = total + bz[s]
    dbo[...] = total / replicas

    for d in x_order[::-1]:
        arrived(tf.at[nx(d)], tfr_s.at[nx(d)], at_x(nx(d)))
    factor = tf[...].reshape(NX * 8, 128)
    both = dot(project, factor, NN, lax.Precision.HIGHEST)
    back[...] = split(both[NX * 8 :])
    qno[...] = both[: NX * 8]

    for qq in range(NQ):
        tgt, copy = to_owner(qq)
        pl.when(z != tgt)(copy.wait_send)

    @pl.when(is_owner)
    def _():
        for d in z_order:
            from_owner(d).wait_send()

    for copy in sent:
        copy.wait_send()


def finish(vo, dto, m, bt, back, qno, dbo, val_h, dt_h, err_h, qn_h, db_h, eo, sem):
    copies = []

    def store(src, dst):
        copy = pltpu.make_async_copy(src, dst, sem.at[len(copies)])
        copy.start()
        copies.append(copy)

    for src, dst in ((dto, dt_h), (vo, val_h), (qno, qn_h), (dbo, db_h)):
        store(src, dst)
    dq = m.shape[0] // NX
    for k in range(NX):
        rows = slice(k * dq, (k + 1) * dq)
        eo[rows, :] = (m[rows, :] - dot(bt[rows, :], back[...], NN)).astype(BF16)
        store(eo.at[pl.ds(k * dq, dq), :], err_h.at[pl.ds(k * dq, dq), :])
    for copy in copies:
        copy.wait()


def per_device(nz, ny, tokens, w_value, b_value, d_values, error_in, q_init):
    rows, d_model = tokens.shape
    head, rank = q_init.shape
    dq = d_model // NX
    dh = dq // 2
    dma = pltpu.SemaphoreType.DMA
    any_spec = pl.BlockSpec(memory_space=pl.ANY)
    hbm = pl.BlockSpec(memory_space=pltpu.HBM)
    vmem = pltpu.VMEM
    scratch = [
        vmem((rows, d_model), BF16), vmem((d_model, head), BF16), vmem((d_model, head), BF16),
        vmem((rows, head), BF16), vmem((rank, head), F32), vmem((1, head), BF16),
        vmem((NX, 2, rank, dh), BF16), vmem((NX, 2, rank, dh), BF16), vmem((2, rank, dh), F32),
        vmem((NQ, 16, dh), BF16), vmem((nz, 16, dh), BF16), vmem((NX, rank, dq), BF16),
        vmem((NX, 2, dh, head), BF16), vmem((2, dh, head), BF16), vmem((2, 2, dh, head), BF16),
        vmem((2 * dq, head), BF16),
        vmem((NX, rank, rank), F32),
        vmem((NX, 8, head), F32), vmem((NX, 8, head), F32), vmem((nz, 8, head), F32), vmem((NX, 8, head), F32),
        vmem((NX, 1, head), F32), vmem((nz, 1, head), F32),
    ]
    scratch += [vmem((ny, 16, d_model), BF16), vmem((ny, 2, 16, d_model), BF16)]
    scratch += [vmem((ny, 16, d_model), BF16)] * 2
    scratch += [
        dma((6,)),
        dma((NX, 2)), dma((2,)), dma((2, 2)), dma((NX,)), dma((NX,)),
        dma((NX, 2)), dma((NX, 2)), dma((NQ,)), dma((nz,)), dma((nz,)), dma((NQ,)), dma((NX,)), dma((NX,)),
        dma((NX,)), dma((NX,)), dma((nz,)), dma((nz,)), dma((NX,)), dma((NX,)),
        dma((NX,)), dma((NX,)), dma((nz,)), dma((nz,)), dma((ny,)), dma((ny,)), dma((ny,)), dma((ny,)),
    ]
    held = pl.BlockSpec(memory_space=pltpu.VMEM)
    operands = (tokens, w_value, b_value.reshape(1, head), d_values, error_in, q_init.T)
    parts = pl.pallas_call(
        functools.partial(kernel, nz, ny),
        out_shape=(
            vmem((rows, head), BF16),
            vmem((16, d_model), BF16),
            vmem((d_model, head), F32),
            vmem((d_model, 2 * rank), BF16),
            vmem((2 * rank, head), BF16),
            vmem((rank, head), F32),
            vmem((1, head), F32),
        ),
        in_specs=[hbm] * 6,
        out_specs=(held,) * 7,
        scratch_shapes=scratch,
        compiler_params=pltpu.CompilerParams(
            collective_id=0, has_side_effects=True, vmem_limit_bytes=48 * 1024 * 1024
        ),
        name="reduce_factors",
    )(*[pltpu.with_memory_space_constraint(a, pltpu.HBM) for a in operands])
    values, d_tokens, error_out, q_next, d_bias = pl.pallas_call(
        finish,
        out_shape=(
            jax.ShapeDtypeStruct((rows, head), BF16),
            jax.ShapeDtypeStruct((16, d_model), BF16),
            jax.ShapeDtypeStruct((d_model, head), BF16),
            jax.ShapeDtypeStruct((rank, head), F32),
            jax.ShapeDtypeStruct((1, head), F32),
        ),
        in_specs=[held] * 7,
        out_specs=(any_spec,) * 5,
        scratch_shapes=[vmem((d_model, head), BF16), dma((8,))],
        compiler_params=pltpu.CompilerParams(vmem_limit_bytes=16 * 1024 * 1024),
        name="store_results",
    )(*parts)
    return values, d_tokens, error_out, q_next.T, d_bias.reshape(head)


def solution(mesh):
    nz = mesh.shape["dp"] // NX
    ny = mesh.shape["tensor"] // 2
    placed = (
        P("dp", None),
        P(None, "tensor"),
        P("tensor"),
        P("dp", "tensor"),
        P("dp", "tensor"),
        P("tensor", None),
    )
    return jax.shard_map(
        functools.partial(per_device, nz, ny),
        mesh=mesh,
        in_specs=placed,
        out_specs=(
            P("dp", "tensor"),
            P(("dp", "tensor"), None),
            P("dp", "tensor"),
            P("tensor", None),
            P("tensor"),
        ),
        check_vma=False,
    )
```

```python
import functools

import jax
import jax.numpy as jnp
from jax import lax
from jax.experimental import pallas as pl
from jax.experimental.pallas import tpu as pltpu
from jax.sharding import PartitionSpec as P

MESH = pl.DeviceIdType.MESH
F32 = jnp.float32
BF16 = jnp.bfloat16
NX = 4
NQ = 4
NN = ((1,), (0,))
NT = ((1,), (1,))
TN = ((0,), (0,))


def dot(a, b, dims, precision=None):
    return lax.dot_general(a, b, (dims, ((), ())), preferred_element_type=F32, precision=precision)


def split(v):
    high = v.astype(BF16)
    low = (v - high.astype(F32)).astype(BF16)
    return jnp.concatenate([high, low], axis=0)


def fold(v):
    n = v.shape[0] // 2
    return v[:n] + v[n:]


def inverse_lower(gram):
    n = gram.shape[0]
    row = lax.broadcasted_iota(jnp.int32, (n, n), 0)
    col = lax.broadcasted_iota(jnp.int32, (n, n), 1)
    a = gram
    inv = (row == col).astype(F32)
    for k in range(0, n, 2):
        col0, col1 = a[:, k : k + 1], a[:, k + 1 : k + 2]
        above = a[k : k + 1, k + 1 : k + 2]
        scale0 = 1.0 / a[k : k + 1, k : k + 1]
        step = a[k + 1 : k + 2, k : k + 1] * scale0
        scale1 = 1.0 / (a[k + 1 : k + 2, k + 1 : k + 2] - step * above)
        factor0 = jnp.where(row[:, :1] > k, col0 * scale0, 0.0)
        factor1 = jnp.where(row[:, :1] > k + 1, (col1 - factor0 * above) * scale1, 0.0)

        def eliminate(v):
            row0, row1 = v[k : k + 1, :], v[k + 1 : k + 2, :]
            return v - factor0 * row0 - factor1 * (row1 - step * row0)

        a, inv = eliminate(a), eliminate(inv)
    pivots = jnp.sum(jnp.where(row == col, a, 0.0), axis=1, keepdims=True)
    return inv / jnp.sqrt(pivots)


def kernel(
    nz, ny,
    tok_h, w_h, b_h, dv_h, e_h, q_h,
    vo, dto, m, bt, back, qno, dbo,
    xv, wv, ev, dvv, qv, bv,
    bxs, bxr, own, zs, zr, bf, ms, rl, mr, mx, gs,
    tsx, trx, tz, tf, bx, bz,
    pr, po, ys, yr,
    in_sem,
    ms_s, rl_r, mr_r, gss_s, gsr_s,
    bxs_s, bxr_s, zs_s, zr_s, ags_s, agr_s, axs_s, axr_s,
    tsx_s, trx_s, tzs_s, tzr_s, tfs_s, tfr_s,
    bias_xs, bias_xr, bias_zs, bias_zr, ps_s, pr_s, ys_s, yr_s,
):
    d_model = wv.shape[0]
    dq = d_model // NX
    dh = dq // 2
    zg = nz // NQ
    replicas = nz * NX
    dp, t = lax.axis_index("dp"), lax.axis_index("tensor")
    z, x = dp // NX, dp % NX
    y, c = t // 2, t % 2
    sib = t + 1 - 2 * c

    def at_x(xx):
        return (z * NX + xx, t)

    def at_z(zz):
        return (zz * NX + x, t)

    def at_y(yy):
        return (dp, yy * 2 + c)

    def nx(d):
        return (x + d) % NX

    def nzz(d):
        return (z + d) % nz

    def nyy(d):
        return (y + d) % ny

    x_order = (2, 1, 3)
    y_order = tuple(sorted(range(1, ny), key=lambda d: -min(d, ny - d)))
    z_order = tuple(sorted(range(1, nz), key=lambda d: -min(d, nz - d)))

    loads = {}
    for i, (name, src, dst) in enumerate(
        (("dv", dv_h, dvv), ("q", q_h, qv), ("e", e_h, ev), ("x", tok_h, xv), ("w", w_h, wv), ("b", b_h, bv))
    ):
        loads[name] = pltpu.make_async_copy(src, dst, in_sem.at[i])
        loads[name].start()

    barrier = pltpu.get_barrier_semaphore()
    peers = [at_x(nx(d)) for d in x_order] + [at_z(nzz(d)) for d in z_order]
    peers += [at_y(nyy(d)) for d in y_order] + [(dp, sib)]
    for peer in peers:
        pl.semaphore_signal(barrier, inc=1, device_id=peer, device_id_type=MESH)

    def remote(src, dst, send, recv, peer):
        return pltpu.make_async_remote_copy(
            src_ref=src, dst_ref=dst, send_sem=send, recv_sem=recv, device_id=peer, device_id_type=MESH
        )

    def arrived(ref, sem, peer):
        remote(ref, ref, sem, sem, peer).wait_recv()

    sent = []

    def send(*args):
        copy = remote(*args)
        copy.start()
        sent.append(copy)

    def columns(j):
        return pl.ds(pl.multiple_of(j * dq, 128), dq)

    loads["dv"].wait()
    loads["q"].wait()
    q_pair = split(qv[...])
    mixed = fold(dot(q_pair, dvv[...], NT))
    mixed_pair = split(mixed)
    loads["e"].wait()
    loads["x"].wait()

    def local_basis(j, half):
        cols = pl.ds(pl.multiple_of(j * dq + half * dh, 128), dh)
        return fold(dot(q_pair, ev[cols, :], NT) + dot(mixed_pair, xv[:, cols], NN))

    for half in range(2):
        for d in x_order:
            bxs[d, half] = local_basis(nx(d), half).astype(BF16)
    pl.semaphore_wait(barrier, len(peers))
    for half in range(2):
        for d in x_order:
            send(
                bxs.at[d, half], bxr.at[x, half], bxs_s.at[d, half], bxr_s.at[x, half], at_x(nx(d))
            )
    for half in range(2):
        own[half] = local_basis(x, half)

    def merged(j):
        cols = columns(j)
        m[cols, :] = dot(xv[:, cols], dvv[...], TN) + ev[cols, :].astype(F32)
        return m[cols, :]

    far = merged(nx(2)).astype(BF16)
    for h, d in ((0, 1), (1, 3)):
        ms[2, h] = far[h * dh : (h + 1) * dh]
        send(ms.at[2, h], rl.at[h], ms_s.at[2, h], rl_r.at[h], at_x(nx(d)))

    owner_pos = (zg - 1) // 2 + c
    mine = z // zg
    is_owner = z % zg == owner_pos

    def to_owner(qq):
        tgt = qq * zg + owner_pos
        return tgt, remote(zs.at[qq], zr.at[z], zs_s.at[qq], zr_s.at[z], at_z(tgt))

    for half in range(2):
        total = own[half]
        for d in x_order[::-1]:
            arrived(bxr.at[nx(d), half], bxr_s.at[nx(d), half], at_x(nx(d)))
            total = total + bxr[nx(d), half].astype(F32)
        for g in range(2):
            qq = 2 * g + half
            zs[qq] = total[16 * g : 16 * g + 16].astype(BF16)
            tgt, copy = to_owner(qq)
            pl.when(z != tgt)(copy.start)

    for h, d in ((0, 1), (1, 3)):
        near = merged(nx(d)).astype(BF16)
        ms[d, 1 - h] = near[(1 - h) * dh : (2 - h) * dh]
        send(ms.at[d, 1 - h], mr.at[h, 1 - h], ms_s.at[d, 1 - h], mr_r.at[h, 1 - h], at_x(nx(d)))

    merged(x)
    for h, d in ((0, 1), (1, 3)):
        arrived(rl.at[h], rl_r.at[h], at_x(nx(4 - d)))
        rows = pl.ds(pl.multiple_of(nx(d) * dq + h * dh, 128), dh)
        ms[d, h] = (m[rows, :] + rl[h].astype(F32)).astype(BF16)
        send(ms.at[d, h], mr.at[h, h], ms_s.at[d, h], mr_r.at[h, h], at_x(nx(d)))

    loads["w"].wait()
    for k in range(NX):
        cols = slice(k * dq, (k + 1) * dq)
        p = dot(dvv[...], wv[cols, :], NT).astype(BF16)
        for yy in range(ny):
            for cc in range(2):
                first = (2 * yy + cc) * 16
                po[yy, cc, :, cols] = p[first : first + 16]
    for yy in range(ny):
        send(po.at[yy, 1 - c], pr.at[yy], ps_s.at[yy], pr_s.at[yy], (dp, sib))

    def block(qq):
        g, half = qq // 2, qq % 2
        return bf.at[x, pl.ds(pl.multiple_of(g * 16, 16), 16), pl.ds(pl.multiple_of(half * dh, 128), dh)]

    def from_owner(d):
        return remote(block(mine), block(mine), ags_s.at[d], agr_s.at[mine], at_z(nzz(d)))

    @pl.when(is_owner)
    def _():
        acc = zs[mine].astype(F32)
        for d in z_order[::-1]:
            arrived(zr.at[nzz(d)], zr_s.at[nzz(d)], at_z(nzz(d)))
            acc = acc + zr[nzz(d)].astype(F32)
        block(mine)[...] = acc.astype(BF16)
        for d in z_order:
            from_owner(d).start()

    bx[x] = jnp.sum(dvv[...].astype(F32), axis=0, keepdims=True)
    for d in x_order:
        send(bx.at[x], bx.at[x], bias_xs.at[d], bias_xr.at[x], at_x(nx(d)))

    loads["b"].wait()
    vo[...] = (dot(xv[...], wv[...], NN) + bv[...].astype(F32)).astype(BF16)

    for d in y_order + (0,):
        yy = nyy(d)
        arrived(pr.at[yy], pr_s.at[yy], (dp, sib))
        ys[yy] = (po[yy, c].astype(F32) + pr[yy].astype(F32)).astype(BF16)
        if d:
            send(ys.at[yy], yr.at[y], ys_s.at[d], yr_s.at[y], at_y(yy))

    for h in range(2):
        total = m[pl.ds(pl.multiple_of(x * dq + h * dh, 128), dh), :]
        for slot, d in ((0, 3), (1, 1)):
            arrived(mr.at[slot, h], mr_r.at[slot, h], at_x(nx(d)))
            total = total + mr[slot, h].astype(F32)
        mx[2 * h * dh : 2 * (h + 1) * dh, :] = split(total)

    for qq in range(NQ):
        tgt = qq * zg + owner_pos

        @pl.when(z != tgt)
        def _():
            arrived(block(qq), agr_s.at[qq], at_z(tgt))

    basis = bf[x]
    factor = sum(
        dot(basis[:, h * dh : (h + 1) * dh], mx[k * dh : (k + 1) * dh, :], NN) for k in range(4) for h in (k // 2,)
    )
    for j in range(NX):
        tsx[j] = factor[8 * j : 8 * j + 8]
    for d in x_order:
        send(tsx.at[nx(d)], trx.at[x], tsx_s.at[d], trx_s.at[x], at_x(nx(d)))
    trx[x] = tsx[x]
    gs[x] = dot(basis, basis, NT)
    for d in x_order:
        send(gs.at[x], gs.at[x], gss_s.at[d], gsr_s.at[x], at_x(nx(d)))
    for d in x_order:
        send(bf.at[x], bf.at[x], axs_s.at[d], axr_s.at[x], at_x(nx(d)))

    for d in x_order[::-1]:
        arrived(trx.at[nx(d)], trx_s.at[nx(d)], at_x(nx(d)))
    tz[z] = (trx[0] + trx[1]) + (trx[2] + trx[3])
    for d in z_order:
        send(tz.at[z], tz.at[z], tzs_s.at[d], tzr_s.at[z], at_z(nzz(d)))

    for d in x_order:
        arrived(bx.at[nx(d)], bias_xr.at[nx(d)], at_x(nx(d)))
    bz[z] = (bx[0] + bx[1]) + (bx[2] + bx[3])
    for d in z_order:
        send(bz.at[z], bz.at[z], bias_zs.at[d], bias_zr.at[z], at_z(nzz(d)))

    for d in x_order[::-1]:
        arrived(gs.at[nx(d)], gsr_s.at[nx(d)], at_x(nx(d)))
    gram = (gs[0] + gs[1]) + (gs[2] + gs[3])
    inv = inverse_lower(gram)
    project = jnp.concatenate([inv, dot(inv, inv, TN, lax.Precision.HIGHEST)], axis=0) / replicas

    def by_rows(j):
        b = bf[j]
        bt[columns(j), :] = jnp.concatenate([b, b], axis=0).T

    by_rows(x)
    for d in z_order[::-1]:
        arrived(tz.at[nzz(d)], tzr_s.at[nzz(d)], at_z(nzz(d)))
    total = tz[0]
    for s in range(1, nz):
        total = total + tz[s]
    tf[x] = total
    for d in x_order:
        send(tf.at[x], tf.at[x], tfs_s.at[d], tfr_s.at[x], at_x(nx(d)))

    for d in x_order[::-1]:
        arrived(bf.at[nx(d)], axr_s.at[nx(d)], at_x(nx(d)))
        by_rows(nx(d))
    acc = ys[y].astype(F32)
    for d in y_order[::-1]:
        arrived(yr.at[nyy(d)], yr_s.at[nyy(d)], at_y(nyy(d)))
        acc = acc + yr[nyy(d)].astype(F32)
    dto[...] = acc.astype(BF16)
    for d in z_order[::-1]:
        arrived(bz.at[nzz(d)], bias_zr.at[nzz(d)], at_z(nzz(d)))
    total = bz[0]
    for s in range(1, nz):
        total = total + bz[s]
    dbo[...] = total / replicas

    for d in x_order[::-1]:
        arrived(tf.at[nx(d)], tfr_s.at[nx(d)], at_x(nx(d)))
    factor = tf[...].reshape(NX * 8, 128)
    both = dot(project, factor, NN, lax.Precision.HIGHEST)
    back[...] = split(both[NX * 8 :])
    qno[...] = both[: NX * 8]

    for qq in range(NQ):
        tgt, copy = to_owner(qq)
        pl.when(z != tgt)(copy.wait_send)

    @pl.when(is_owner)
    def _():
        for d in z_order:
            from_owner(d).wait_send()

    for copy in sent:
        copy.wait_send()


def finish(vo, dto, m, bt, back, qno, dbo, val_h, dt_h, err_h, qn_h, db_h, eo, sem):
    copies = []

    def store(src, dst):
        copy = pltpu.make_async_copy(src, dst, sem.at[len(copies)])
        copy.start()
        copies.append(copy)

    for src, dst in ((dto, dt_h), (vo, val_h), (qno, qn_h), (dbo, db_h)):
        store(src, dst)
    dq = m.shape[0] // NX
    for k in range(NX):
        rows = slice(k * dq, (k + 1) * dq)
        eo[rows, :] = (m[rows, :] - dot(bt[rows, :], back[...], NN)).astype(BF16)
        store(eo.at[pl.ds(k * dq, dq), :], err_h.at[pl.ds(k * dq, dq), :])
    for copy in copies:
        copy.wait()


def per_device(nz, ny, tokens, w_value, b_value, d_values, error_in, q_init):
    rows, d_model = tokens.shape
    head, rank = q_init.shape
    dq = d_model // NX
    dh = dq // 2
    dma = pltpu.SemaphoreType.DMA
    any_spec = pl.BlockSpec(memory_space=pl.ANY)
    hbm = pl.BlockSpec(memory_space=pltpu.HBM)
    vmem = pltpu.VMEM
    scratch = [
        vmem((rows, d_model), BF16), vmem((d_model, head), BF16), vmem((d_model, head), BF16),
        vmem((rows, head), BF16), vmem((rank, head), F32), vmem((1, head), BF16),
        vmem((NX, 2, rank, dh), BF16), vmem((NX, 2, rank, dh), BF16), vmem((2, rank, dh), F32),
        vmem((NQ, 16, dh), BF16), vmem((nz, 16, dh), BF16), vmem((NX, rank, dq), BF16),
        vmem((NX, 2, dh, head), BF16), vmem((2, dh, head), BF16), vmem((2, 2, dh, head), BF16),
        vmem((2 * dq, head), BF16),
        vmem((NX, rank, rank), F32),
        vmem((NX, 8, head), F32), vmem((NX, 8, head), F32), vmem((nz, 8, head), F32), vmem((NX, 8, head), F32),
        vmem((NX, 1, head), F32), vmem((nz, 1, head), F32),
    ]
    scratch += [vmem((ny, 16, d_model), BF16), vmem((ny, 2, 16, d_model), BF16)]
    scratch += [vmem((ny, 16, d_model), BF16)] * 2
    scratch += [
        dma((6,)),
        dma((NX, 2)), dma((2,)), dma((2, 2)), dma((NX,)), dma((NX,)),
        dma((NX, 2)), dma((NX, 2)), dma((NQ,)), dma((nz,)), dma((nz,)), dma((NQ,)), dma((NX,)), dma((NX,)),
        dma((NX,)), dma((NX,)), dma((nz,)), dma((nz,)), dma((NX,)), dma((NX,)),
        dma((NX,)), dma((NX,)), dma((nz,)), dma((nz,)), dma((ny,)), dma((ny,)), dma((ny,)), dma((ny,)),
    ]
    held = pl.BlockSpec(memory_space=pltpu.VMEM)
    operands = (tokens, w_value, b_value.reshape(1, head), d_values, error_in, q_init.T)
    parts = pl.pallas_call(
        functools.partial(kernel, nz, ny),
        out_shape=(
            vmem((rows, head), BF16),
            vmem((16, d_model), BF16),
            vmem((d_model, head), F32),
            vmem((d_model, 2 * rank), BF16),
            vmem((2 * rank, head), BF16),
            vmem((rank, head), F32),
            vmem((1, head), F32),
        ),
        in_specs=[hbm] * 6,
        out_specs=(held,) * 7,
        scratch_shapes=scratch,
        compiler_params=pltpu.CompilerParams(
            collective_id=0, has_side_effects=True, vmem_limit_bytes=48 * 1024 * 1024
        ),
        name="reduce_factors",
    )(*[pltpu.with_memory_space_constraint(a, pltpu.HBM) for a in operands])
    values, d_tokens, error_out, q_next, d_bias = pl.pallas_call(
        finish,
        out_shape=(
            jax.ShapeDtypeStruct((rows, head), BF16),
            jax.ShapeDtypeStruct((16, d_model), BF16),
            jax.ShapeDtypeStruct((d_model, head), BF16),
            jax.ShapeDtypeStruct((rank, head), F32),
            jax.ShapeDtypeStruct((1, head), F32),
        ),
        in_specs=[held] * 7,
        out_specs=(any_spec,) * 5,
        scratch_shapes=[vmem((d_model, head), BF16), dma((8,))],
        compiler_params=pltpu.CompilerParams(vmem_limit_bytes=16 * 1024 * 1024),
        name="store_results",
    )(*parts)
    return values, d_tokens, error_out, q_next.T, d_bias.reshape(head)


def solution(mesh):
    nz = mesh.shape["dp"] // NX
    ny = mesh.shape["tensor"] // 2
    placed = (
        P("dp", None),
        P(None, "tensor"),
        P("tensor"),
        P("dp", "tensor"),
        P("dp", "tensor"),
        P("tensor", None),
    )
    return jax.shard_map(
        functools.partial(per_device, nz, ny),
        mesh=mesh,
        in_specs=placed,
        out_specs=(
            P("dp", "tensor"),
            P(("dp", "tensor"), None),
            P("dp", "tensor"),
            P("tensor", None),
            P("tensor"),
        ),
        check_vma=False,
    )
```
